32 devices in a mesh: tx: 16 (over z, y, x), ty: 2 (over core).
Axes of the slice: x: 2, y: 2, z: 4, core: 2. Of those that a mesh axis runs over, the one named last changes fastest.
Arguments:
- forcing: float32 [3, 6, 256, 256], P(None, None, 'tx', 'ty'), may hold values from -6 to 6
- start_state: float32 [3, 6, 256, 256], P(None, None, 'tx', 'ty'), may hold values from -4 to 4
- ice_mask: int32 [256, 256], P('tx', 'ty'), may hold values from 0 to 2
- class_ids: int32 [6, 256, 256], P(None, 'tx', 'ty'), may hold values from 0 to 15
- eta_table: float32 [16], replicated, may hold values from 0.1 to 10
- friction: float32 [256, 256], P('tx', 'ty'), may hold values from 0.3 to 30
Outputs:
- adjoint: float32 [3, 6, 256, 256], P(None, None, 'tx', 'ty')
- residual: float32 [3, 6, 256, 256], P(None, None, 'tx', 'ty')
The draws below stay inside these ranges and needn't reach their ends.
Inputs may be any that keep to these rules, and one draw needn't show every extreme that they name: `ice_mask`: 0 marks an ocean column, 1 a grounded one, 2 a floating one. `class_ids`: an index into eta_table.
All inputs are finite; a program needn't handle non-finite values.
Results may differ from the reference program's by a relative error of at most 0.00002.
Values sent between devices are 32-bit elements; how exact they have to be, the bound alone decides.
No kernel may reach another device: no remote copies, remote signals or barrier semaphores. Data moves between devices by JAX's collectives and lax.ppermute only.
A program may use at most 64 MiB of HBM per device.

```python
import math
import jax
import jax.numpy as jnp
from jax import lax

NZ = 6
NCLASS = 16
SWEEPS = 2
COARSE_SWEEPS = 4
NX = 256
NY = 256


def place_ends(result, rng, smallest, largest):
    longest = result.shape.index(max(result.shape))
    spots = []
    for shift in (0, 1):
        where = [jax.random.randint(jax.random.fold_in(rng, axis), (), 0, length) for axis, length in enumerate(result.shape)]
        where[longest] = (where[longest] + shift) % result.shape[longest]
        spots.append(tuple(where))
    return result.at[spots[0]].set(smallest).at[spots[1]].set(largest)


def block_levels(rng, dims, shards, smallest, high):
    def one(position, parts):
        steps = jax.random.uniform(jax.random.fold_in(jax.random.fold_in(rng, 6), position), (parts,), jnp.float32, smallest / len(shards), high / len(shards))
        return jnp.repeat(jnp.exp(steps), dims[position] // parts).reshape((-1,) + (1,) * (len(dims) - position - 1))

    level = one(*shards[0])
    for cut in shards[1:]:
        level = level * one(*cut)
    return level


def noise(stream_key, extent, scale, limit, cuts=(), held_as=jnp.bfloat16):
    factor_of = block_levels(stream_key, extent, cuts, -0.22, 0.18) if cuts else 1.0
    drawn = jax.random.normal(stream_key, extent, jnp.float32) * scale * factor_of
    return jnp.minimum(jnp.maximum(drawn, -limit), limit).astype(held_as)


def setup_inputs(seed: int = 0) -> dict:
    key_list = jax.random.split(jax.random.key(seed), 7)
    forcing = noise(key_list[0], (3, NZ, NX, NY), 1.0, 6.0, ((2, 16), (3, 2)), jnp.float32)
    start_state = noise(key_list[1], (3, NZ, NX, NY), 0.5, 4.0, ((2, 16), (3, 2)), jnp.float32)
    ice_mask = place_ends(jax.random.randint(key_list[2], (NX, NY), 0, 3), jax.random.fold_in(key_list[2], 1), 0, 2).astype(jnp.int32)
    class_ids = place_ends(jax.random.randint(key_list[3], (NZ, NX, NY), 0, NCLASS), jax.random.fold_in(key_list[3], 1), 0, NCLASS - 1).astype(jnp.int32)
    eta_table = jnp.clip(jnp.exp(jax.random.uniform(key_list[4], (NCLASS,), jnp.float32, math.log(0.1), math.log(10.0))), 0.1, 10.0)
    friction = jnp.clip(jnp.exp(math.log(30.0) - 4.6051701 * jax.random.uniform(key_list[5], (NX, NY), jnp.float32) ** block_levels(key_list[5], (NX, NY), ((0, 16), (1, 2)), -0.2, 0.2)), 0.3, 30.0)
    return {"forcing": forcing, "start_state": start_state, "ice_mask": ice_mask, "class_ids": class_ids, "eta_table": eta_table, "friction": friction}


DAMPING = 0.6
VERTICAL = 2.0
REACTION = 0.05


def stencil_terms():
    terms = []
    for step_z in (-1, 0, 1):
        for step_x in (-1, 0, 1):
            for step_y in (-1, 0, 1):
                nonzero_axes = abs(step_z) + abs(step_x) + abs(step_y)
                if nonzero_axes > 0:
                    terms.append((step_z, step_x, step_y, nonzero_axes))
    return terms


def apply_operator(padded, coef_pad, spacing, ocean_weight):
    layers = padded.shape[1]
    width_x = padded.shape[2] - 2
    width_y = padded.shape[3] - 2
    viscosity = coef_pad[:layers]
    active = jnp.broadcast_to(coef_pad[layers], viscosity.shape)
    basal = coef_pad[layers + 1]
    visc_z = jnp.pad(viscosity, ((1, 1), (0, 0), (0, 0)))
    active_z = jnp.pad(active, ((1, 1), (0, 0), (0, 0)))
    field_z = jnp.pad(padded, ((0, 0), (1, 1), (0, 0), (0, 0)))
    visc_mid = viscosity[:, 1:1 + width_x, 1:1 + width_y]
    active_mid = active[:, 1:1 + width_x, 1:1 + width_y]
    coupled = jnp.zeros((3, layers, width_x, width_y), jnp.float32)
    weight_sum = jnp.zeros((3, layers, width_x, width_y), jnp.float32)
    for step_z, step_x, step_y, nonzero_axes in stencil_terms():
        base_weight = (0.25 ** (nonzero_axes - 1)) * (VERTICAL ** abs(step_z)) * (spacing ** (abs(step_x) + abs(step_y)))
        factors = jnp.array([1.0 + abs(step_x), 1.0 + abs(step_y), 1.0 + abs(step_z)], jnp.float32).reshape(3, 1, 1, 1) * base_weight
        z_range = slice(1 + step_z, 1 + step_z + layers)
        x_range = slice(1 + step_x, 1 + step_x + width_x)
        y_range = slice(1 + step_y, 1 + step_y + width_y)
        pair_mean = 0.5 * (visc_mid + visc_z[z_range, x_range, y_range]) * active_mid * active_z[z_range, x_range, y_range]
        links = factors * pair_mean[None]
        coupled = coupled + links * field_z[:, z_range, x_range, y_range]
        weight_sum = weight_sum + links
    layer_ids = lax.broadcasted_iota(jnp.int32, (3, layers, 1, 1), 1)
    comp_ids = lax.broadcasted_iota(jnp.int32, (3, layers, 1, 1), 0)
    bottom = jnp.where((layer_ids == 0) & (comp_ids < 2), 1.0, 0.0).astype(jnp.float32)
    basal_term = bottom * basal[None, None, 1:1 + width_x, 1:1 + width_y]
    diagonal = weight_sum + (REACTION * visc_mid * active_mid + ocean_weight * (1.0 - active_mid))[None] + basal_term
    centre = padded[:, :, 1:1 + width_x, 1:1 + width_y]
    return diagonal * centre - coupled, diagonal


def jacobi_sweep(padded, right_side, coef_pad, spacing, ocean_weight):
    applied, diagonal = apply_operator(padded, coef_pad, spacing, ocean_weight)
    centre = padded[:, :, 1:-1, 1:-1]
    return centre + DAMPING * (right_side - applied) / diagonal


def build_coefficients(class_ids, eta_table, ice_mask, friction):
    levels = lax.broadcasted_iota(jnp.int32, (eta_table.shape[0], 1, 1, 1), 0)
    viscosity = jnp.sum(jnp.where(class_ids[None] == levels, eta_table[:, None, None, None], 0.0), axis=0)
    active = jnp.where(ice_mask != 0, 1.0, 0.0).astype(jnp.float32)
    basal = jnp.where(ice_mask == 1, friction, 0.0)
    return jnp.concatenate([viscosity, active[None], basal[None]], axis=0)


def coarsen_sum(values):
    leading = values.shape[:-2]
    shaped = values.reshape(leading + (values.shape[-2] // 2, 2, values.shape[-1] // 2, 2))
    return jnp.sum(shaped, axis=(-3, -1))


def coarse_coefficients(coefficients):
    layers = coefficients.shape[0] - 2
    summed = coarsen_sum(coefficients)
    return jnp.concatenate([summed[:layers], 0.25 * summed[layers:layers + 1], summed[layers + 1:]], axis=0)


def refine(values):
    return jnp.repeat(jnp.repeat(values, 2, axis=-2), 2, axis=-1)


def pad_grid(values):
    return jnp.pad(values, ((0, 0), (0, 0), (1, 1), (1, 1)))


def reference(forcing, start_state, ice_mask, class_ids, eta_table, friction):
    coefficients = build_coefficients(class_ids, eta_table, ice_mask, friction)
    coef_pad = jnp.pad(coefficients, ((0, 0), (1, 1), (1, 1)))
    iterate = start_state
    for sweep_index in range(SWEEPS):
        iterate = jacobi_sweep(pad_grid(iterate), forcing, coef_pad, 1.0, 1.0)
    applied, unused_diag = apply_operator(pad_grid(iterate), coef_pad, 1.0, 1.0)
    fine_residual = forcing - applied
    coarse_rhs = coarsen_sum(fine_residual)
    coarse_pad = jnp.pad(coarse_coefficients(coefficients), ((0, 0), (1, 1), (1, 1)))
    correction = jnp.zeros_like(coarse_rhs)
    for sweep_index in range(COARSE_SWEEPS):
        correction = jacobi_sweep(pad_grid(correction), coarse_rhs, coarse_pad, 0.5, 4.0)
    iterate = iterate + refine(correction)
    for sweep_index in range(SWEEPS):
        iterate = jacobi_sweep(pad_grid(iterate), forcing, coef_pad, 1.0, 1.0)
    applied, unused_diag = apply_operator(pad_grid(iterate), coef_pad, 1.0, 1.0)
    return iterate, forcing - applied
```

```python
import functools

import jax
import jax.numpy as jnp
from jax import lax
from jax.experimental import pallas as pl
from jax.experimental.pallas import tpu as pltpu
from jax.sharding import PartitionSpec as P

DAMPING = 0.6
REACTION = 0.05
F32 = jnp.float32
VMEM = pl.BlockSpec(memory_space=pltpu.VMEM)
SMEM = pl.BlockSpec(memory_space=pltpu.SMEM)
PARAMS = pltpu.CompilerParams(vmem_limit_bytes=16 * 2**20)

REACH, REACH_RHS, REACH_CRHS, REACH_CCOEF = 3, 2, 5, 6


def along_x(block_a, block_b, sizes):
    count, width = sizes
    pairs = []
    for core in range(width):
        step = [(i * width + core, (i + 1) * width + core) for i in range(count - 1)]
        pairs += step if core % 2 == 0 else [(b, a) for a, b in step]
    if width % 2 == 0:
        for core in range(0, width, 2):
            last = (count - 1) * width
            pairs += [(last + core, last + core + 1), (core + 1, core)]
    back = [(b, a) for a, b in pairs]
    return (
        lax.ppermute(block_a, ("tx", "ty"), pairs),
        lax.ppermute(block_b, ("tx", "ty"), back),
    )


def along_y(block, sizes):
    width = sizes[1]
    if width == 1:
        return jnp.zeros_like(block)
    if width == 2:
        return lax.ppermute(block, "ty", [(0, 1), (1, 0)])
    following = lax.ppermute(block, "ty", [(j + 1, j) for j in range(width - 1)])
    previous = lax.ppermute(block, "ty", [(j, j + 1) for j in range(width - 1)])
    lane = lax.broadcasted_iota(jnp.int32, block.shape, block.ndim - 1)
    return jnp.where(lane < block.shape[-1] // 2, following, previous)


def filter_x(value, weight):
    rows = value.shape[0]
    return value + weight * (pltpu.roll(value, 1, 0) + pltpu.roll(value, rows - 1, 0))


def filter_y(pair, weight, step):
    own, halo = pair
    lanes = own.shape[1]
    lane = lax.broadcasted_iota(jnp.int32, own.shape, 1)
    low = lane < step
    high = lane >= lanes - step
    own_low, halo_low = pltpu.roll(own, step, 1), pltpu.roll(halo, step, 1)
    own_high, halo_high = pltpu.roll(own, lanes - step, 1), pltpu.roll(halo, lanes - step, 1)
    new_own = jnp.where(low, halo_low, own_low) + jnp.where(high, halo_high, own_high)
    new_halo = jnp.where(low, own_low, halo_low) + jnp.where(high, own_high, halo_high)
    return own + weight * new_own, halo + weight * new_halo


def filter_z(values, z, weight):
    total = None
    for other in (z - 1, z + 1):
        if 0 <= other < len(values):
            total = values[other] if total is None else total + values[other]
    return values[z] + weight * total


def coupling(c, u, v, va, a, spacing, step):
    layers = len(u)
    wx, wy, wz = (
        jnp.where(c == axis, 2.0, 1.0).astype(F32) * base
        for axis, base in ((0, 0.25 * spacing), (1, 0.25 * spacing), (2, 0.5))
    )
    q = [[va[z][t] * u[z][t] for t in (0, 1)] for z in range(layers)]
    result = []
    for z in range(layers):
        sp, sq = [], []
        for t in (0, 1):
            sp.append(filter_x(a[t] * filter_z([w[t] for w in u], z, wz), wx))
            sq.append(filter_x(filter_z([w[t] for w in q], z, wz), wx))
        sp, sq = filter_y(sp, wy, step), filter_y(sq, wy, step)
        result.append([v[z][t] * sp[t] + sq[t] - 2.0 * q[z][t] for t in (0, 1)])
    return result


def layers_of(ref, c, layers):
    return [[ref[t, c, z] for t in (0, 1)] for z in range(layers)]


def fields_of(ref, layers):
    return [[ref[t, z] for t in (0, 1)] for z in range(layers)]


def build_diagonal(v, va, a, basal, spacing, step, ocean, write):
    layers = len(v)
    ones = [[jnp.ones_like(a[t]) for t in (0, 1)] for _ in range(layers)]

    def component(c, carry):
        terms = coupling(c, ones, v, va, a, spacing, step)
        grounded = jnp.where(c < 2, 1.0, 0.0).astype(F32)
        for z in range(layers):
            for t in (0, 1):
                diagonal = 2.0 * a[t] * terms[z][t] + REACTION * va[z][t] + ocean * (1.0 - a[t])
                if z == 0:
                    diagonal = diagonal + grounded * basal[t]
                write(t, c, z, diagonal)
        return carry

    lax.fori_loop(0, 3, component, 0)


def sweep(source, target, gain, rhs, v_ref, va_ref, a_ref, layers, spacing, step):
    def component(c, carry):
        a = [a_ref[t] for t in (0, 1)]
        u = layers_of(source, c, layers)
        terms = coupling(c, u, fields_of(v_ref, layers), fields_of(va_ref, layers), a, spacing, step)
        for z in range(layers):
            for t in (0, 1):
                applied = rhs[t, c, z] + 2.0 * a[t] * terms[z][t]
                target[t, c, z] = (1.0 - DAMPING) * u[z][t] + gain[t, c, z] * applied
        return carry

    lax.fori_loop(0, 3, component, 0)


def residual(source, rhs, diag, v_ref, va_ref, a_ref, layers, rows, tiles, write):
    def component(c, carry):
        a = [a_ref[t] for t in (0, 1)]
        u = layers_of(source, c, layers)
        terms = coupling(c, u, fields_of(v_ref, layers), fields_of(va_ref, layers), a, 1.0, 1)
        for z in range(layers):
            for t in range(tiles):
                applied = rhs[t, c, z] + 2.0 * a[t] * terms[z][t]
                write(t, c, z, applied[:rows] - diag[t, c, z, :rows] * u[z][t][:rows])
        return carry

    lax.fori_loop(0, 3, component, 0)


def inside(rows, own_rows, lanes, sizes):
    i, j = lax.axis_index("tx"), lax.axis_index("ty")
    below = jnp.where(i < sizes[0] - 1, 1.0, 0.0).astype(F32)
    above = jnp.where(i > 0, 1.0, 0.0).astype(F32)
    after = jnp.where(j < sizes[1] - 1, 1.0, 0.0).astype(F32)
    before = jnp.where(j > 0, 1.0, 0.0).astype(F32)
    row = lax.broadcasted_iota(jnp.int32, (rows, lanes), 0)
    lane = lax.broadcasted_iota(jnp.int32, (rows, lanes), 1)
    middle = own_rows + (rows - own_rows) // 2
    by_row = jnp.where(row < own_rows, 1.0, jnp.where(row < middle, below, above))
    by_lane = jnp.where(lane < lanes // 2, after, before)
    return by_row, by_row * by_lane


def sort_sides(blocks, partner_blocks, sides):
    even = lax.axis_index("ty") % 2 == 0
    first, second = blocks[0][...], blocks[1][...]
    sides[0, 0] = jnp.where(even, first, second)
    sides[0, 1] = jnp.where(even, second, first)
    first, second = partner_blocks[0][...], partner_blocks[1][...]
    sides[1, 0] = jnp.where(even, second, first)
    sides[1, 1] = jnp.where(even, first, second)


def write_messages(forward, backward, out_a, out_b):
    even = lax.axis_index("ty") % 2 == 0
    first, second = forward[...], backward[...]
    out_a[...] = jnp.where(even, first, second)
    out_b[...] = jnp.where(even, second, first)


def pack_kernel(start, forcing, mask, classes, eta, friction, out_a, out_b, coef, ends):
    layers, rows = classes.shape[:2]
    fields = 3 * layers
    ids = classes[...]
    viscosity = jnp.zeros(classes.shape, F32)
    for k in range(eta.shape[0]):
        viscosity = jnp.where(ids == k, eta[k], viscosity)
    coef[:layers] = viscosity
    kind = mask[...]
    coef[layers] = jnp.where(kind != 0, 1.0, 0.0).astype(F32)
    coef[layers + 1] = jnp.where(kind == 1, friction[...], 0.0)
    for side in (0, 1):
        def edge(ref, reach, *index):
            first = rows - reach if side == 0 else 0
            return ref[(*index, slice(first, first + reach))]

        place = 0
        for f in range(fields):
            ends[side, place : place + REACH] = edge(start, REACH, f // layers, f % layers)
            place += REACH
        for f in range(fields):
            ends[side, place : place + REACH_RHS] = edge(forcing, REACH_RHS, f // layers, f % layers)
            place += REACH_RHS
        for f in range(layers + 2):
            ends[side, place : place + REACH] = edge(coef, REACH, f)
            place += REACH
    write_messages(ends.at[0], ends.at[1], out_a, out_b)


def presmooth_kernel(
    sizes,
    start, start_n, forcing, forcing_n, coef, coef_n, in_a, in_b, in_an, in_bn,
    pre, crhs, ccoef, rhs, v, va, a, gain, diag, out_a, out_b,
    sides, u0, u1, res, basal, ends,
):
    layers, rows, lanes = start.shape[1:]
    total = rows + 8
    half = rows // 2
    fields = 3 * layers
    sort_sides((in_a, in_b), (in_an, in_bn), sides)

    def fill(target, own, reach, place, *index):
        t = index[0]
        target[(*index, slice(0, rows))] = own
        target[(*index, slice(rows, total))] = jnp.zeros((8, lanes), F32)
        target[(*index, slice(rows, rows + reach))] = sides[t, 1, place : place + reach]
        target[(*index, slice(total - reach, total))] = sides[t, 0, place : place + reach]

    valid = inside(total, rows, lanes, sizes)
    for t in (0, 1):
        s, g, k = ((start, forcing, coef), (start_n, forcing_n, coef_n))[t]
        place = 0
        for f in range(fields):
            c, z = f // layers, f % layers
            fill(u0, s[c, z], REACH, place, t, c, z)
            place += REACH
        for f in range(fields):
            c, z = f // layers, f % layers
            fill(rhs, g[c, z], REACH_RHS, place, t, c, z)
            place += REACH_RHS
        for z in range(layers):
            fill(v, k[z], REACH, place, t, z)
            place += REACH
        fill(a, k[layers], REACH, place, t)
        fill(basal, k[layers + 1], REACH, place + REACH, t)
        a[t] = a[t] * valid[t]
        for z in range(layers):
            va[t, z] = v[t, z] * a[t]

    def keep(t, c, z, diagonal):
        diag[t, c, z] = diagonal
        gain[t, c, z] = DAMPING / diagonal

    pairs_a = [a[t] for t in (0, 1)]
    build_diagonal(
        fields_of(v, layers), fields_of(va, layers), pairs_a,
        [basal[t] for t in (0, 1)], 1.0, 1, 1.0, keep,
    )
    sweep(u0, u1, gain, rhs, v, va, a, layers, 1.0, 1)
    sweep(u1, u0, gain, rhs, v, va, a, layers, 1.0, 1)

    def put(t, c, z, value):
        res[t, c, z] = value

    residual(u0, rhs, diag, v, va, a, layers, rows, 2, put)
    for t in (0, 1):
        for c in range(3):
            for z in range(layers):
                pre[t, c, z] = u0[t, c, z, :rows]

    even = lax.broadcasted_iota(jnp.int32, (half, lanes), 1) % 2 == 0

    def coarsen(ref, *index):
        summed = ref[(*index, pl.ds(0, half, 2))] + ref[(*index, pl.ds(1, half, 2))]
        return summed + jnp.where(even, pltpu.roll(summed, lanes - 1, 1), pltpu.roll(summed, 1, 1))

    for t in (0, 1):
        for c in range(3):
            for z in range(layers):
                crhs[t, c, z] = coarsen(res, t, c, z)
        for z in range(layers):
            ccoef[t, z] = coarsen(v, t, z)
        ccoef[t, layers] = 0.25 * coarsen(a, t)
        ccoef[t, layers + 1] = coarsen(basal, t)

    for side in (0, 1):
        first = rows - REACH if side == 0 else 0
        place = 0
        for f in range(fields):
            ends[side, place : place + REACH] = u0[0, f // layers, f % layers, first : first + REACH]
            place += REACH

        def edge(value, reach):
            return value[half - reach :] if side == 0 else value[:reach]

        for f in range(0, fields, 2):
            one = crhs[0, f // layers, f % layers]
            two = crhs[0, (f + 1) // layers, (f + 1) % layers]
            ends[side, place : place + REACH_CRHS] = edge(jnp.where(even, one, two), REACH_CRHS)
            place += REACH_CRHS
        for f in range(0, layers + 2, 2):
            both = jnp.where(even, ccoef[0, f], ccoef[0, f + 1])
            ends[side, place : place + REACH_CCOEF] = edge(both, REACH_CCOEF)
            place += REACH_CCOEF
    write_messages(ends.at[0], ends.at[1], out_a, out_b)


def coarse_kernel(
    sizes,
    pre, crhs, ccoef, rhs, v, va, a, gain, diag, in_a, in_b, in_an, in_bn,
    adjoint, final,
    sides, u0, u1, cr, cv, cva, ca, cgain, c0, c1, wide,
):
    layers, rows, lanes = pre.shape[2:]
    total = rows + 8
    half = rows // 2
    ctotal = half + 16
    fields = 3 * layers
    sort_sides((in_a, in_b), (in_an, in_bn), sides)
    place_r = REACH * fields
    place_c = place_r + REACH_CRHS * (fields // 2)
    even = lax.broadcasted_iota(jnp.int32, (8, lanes), 1) % 2 == 0

    def unpack(t, side, place, reach):
        both = sides[t, side, place : place + reach]
        first = even[:reach]
        return (
            jnp.where(first, both, pltpu.roll(both, 1, 1)),
            jnp.where(first, pltpu.roll(both, lanes - 1, 1), both),
        )

    def fill(target, own, above, below, *index):
        reach = above.shape[0]
        target[(*index, slice(0, half))] = own
        target[(*index, slice(half, ctotal))] = jnp.zeros((16, lanes), F32)
        target[(*index, slice(half, half + reach))] = below
        target[(*index, slice(ctotal - reach, ctotal))] = above

    valid = inside(ctotal, half, lanes, sizes)
    for t in (0, 1):
        for m in range(fields // 2):
            above = unpack(t, 0, place_r + REACH_CRHS * m, REACH_CRHS)
            below = unpack(t, 1, place_r + REACH_CRHS * m, REACH_CRHS)
            for k in (0, 1):
                c, z = (2 * m + k) // layers, (2 * m + k) % layers
                fill(cr, crhs[t, c, z], above[k], below[k], t, c, z)
        for m in range(layers // 2 + 1):
            above = unpack(t, 0, place_c + REACH_CCOEF * m, REACH_CCOEF)
            below = unpack(t, 1, place_c + REACH_CCOEF * m, REACH_CCOEF)
            for k in (0, 1):
                f = 2 * m + k
                fill(cv, ccoef[t, f], above[k], below[k], t, f)
        ca[t] = cv[t, layers] * valid[t]
        for z in range(layers):
            cva[t, z] = cv[t, z] * ca[t]

    def keep(t, c, z, diagonal):
        value = DAMPING / diagonal
        cgain[t, c, z] = value
        c0[t, c, z] = value * cr[t, c, z]

    build_diagonal(
        fields_of(cv, layers), fields_of(cva, layers), [ca[t] for t in (0, 1)],
        [cv[t, layers + 1] for t in (0, 1)], 0.5, 2, 4.0, keep,
    )
    sweep(c0, c1, cgain, cr, cv, cva, ca, layers, 0.5, 2)
    sweep(c1, c0, cgain, cr, cv, cva, ca, layers, 0.5, 2)
    sweep(c0, c1, cgain, cr, cv, cva, ca, layers, 0.5, 2)

    for t in (0, 1):
        for c in range(3):
            for z in range(layers):
                place = REACH * (c * layers + z)
                u0[t, c, z, :rows] = pre[t, c, z]
                u0[t, c, z, rows:] = jnp.zeros((8, lanes), F32)
                u0[t, c, z, rows : rows + REACH] = sides[t, 1, place : place + REACH]
                u0[t, c, z, total - REACH :] = sides[t, 0, place : place + REACH]
                for phase in (0, 1):
                    wide[pl.ds(phase, half, 2)] = c1[t, c, z, :half]
                    wide[pl.ds(rows + phase, 2, 2)] = c1[t, c, z, half : half + 2]
                    wide[pl.ds(rows + 4 + phase, 2, 2)] = c1[t, c, z, ctotal - 2 :]
                u0[t, c, z] = u0[t, c, z] + wide[...]
    sweep(u0, u1, gain, rhs, v, va, a, layers, 1.0, 1)
    sweep(u1, u0, gain, rhs, v, va, a, layers, 1.0, 1)

    def put(t, c, z, value):
        final[c, z] = value

    residual(u0, rhs, diag, v, va, a, layers, rows, 1, put)
    for c in range(3):
        for z in range(layers):
            adjoint[c, z] = u0[0, c, z, :rows]


def shards(sizes, forcing, start_state, ice_mask, class_ids, eta_table, friction):
    layers, rows, lanes = start_state.shape[1:]
    total, half = rows + 8, rows // 2
    ctotal = half + 16

    def shape(*dims):
        return jax.ShapeDtypeStruct(dims, F32)

    def message(count):
        return shape(-(-count // 8) * 8, lanes)

    def call(body, outs, scratch, *operands):
        specs = [VMEM] * len(operands)
        if body is pack_kernel:
            specs[4] = SMEM
        return pl.pallas_call(
            body,
            out_shape=outs,
            in_specs=specs,
            out_specs=[VMEM] * len(outs),
            scratch_shapes=[pltpu.VMEM(s.shape, F32) for s in scratch],
            compiler_params=PARAMS,
        )(*operands)

    first = message(3 * layers * (REACH + REACH_RHS) + (layers + 2) * REACH)
    second = message(
        3 * layers * REACH + 3 * layers // 2 * REACH_CRHS + (layers + 2) // 2 * REACH_CCOEF
    )

    def both(block):
        return shape(2, *block.shape)

    start_n, forcing_n = along_y(start_state, sizes), along_y(forcing, sizes)
    block_a, block_b, coef = call(
        pack_kernel,
        [first, first, shape(layers + 2, rows, lanes)],
        [both(first)],
        start_state, forcing, ice_mask, class_ids, eta_table, friction,
    )
    in_a, in_b = along_x(block_a, block_b, sizes)
    coef_n = along_y(coef, sizes)
    in_an, in_bn = along_y(in_a, sizes), along_y(in_b, sizes)
    level = shape(2, 3, layers, total, lanes)
    columns = shape(2, layers, total, lanes)
    plane = shape(2, total, lanes)
    *kept, block_a, block_b = call(
        functools.partial(presmooth_kernel, sizes),
        [
            shape(2, 3, layers, rows, lanes),
            shape(2, 3, layers, half, lanes),
            shape(2, layers + 2, half, lanes),
            level, columns, columns, plane, level, level,
            second, second,
        ],
        [both(both(first)), level, level, shape(2, 3, layers, rows, lanes), plane, both(second)],
        start_state, start_n, forcing, forcing_n, coef, coef_n, in_a, in_b, in_an, in_bn,
    )
    in_a, in_b = along_x(block_a, block_b, sizes)
    in_an, in_bn = along_y(in_a, sizes), along_y(in_b, sizes)
    clevel = shape(2, 3, layers, ctotal, lanes)
    own = shape(3, layers, rows, lanes)
    return call(
        functools.partial(coarse_kernel, sizes),
        [own, own],
        [
            both(both(second)), level, level, clevel,
            shape(2, layers + 2, ctotal, lanes), shape(2, layers, ctotal, lanes),
            shape(2, ctotal, lanes), clevel, clevel, clevel, shape(total, lanes),
        ],
        *kept, in_a, in_b, in_an, in_bn,
    )


def solution(mesh):
    sizes = (mesh.shape["tx"], mesh.shape["ty"])

    def block(*operands):
        return tuple(shards(sizes, *operands))

    return jax.shard_map(
        block,
        mesh=mesh,
        in_specs=(
            P(None, None, "tx", "ty"),
            P(None, None, "tx", "ty"),
            P("tx", "ty"),
            P(None, "tx", "ty"),
            P(),
            P("tx", "ty"),
        ),
        out_specs=(P(None, None, "tx", "ty"), P(None, None, "tx", "ty")),
        check_vma=False,
    )
```
